32 devices in a mesh: panel: 8 (over y, x, core), col: 4 (over z).
Axes of the slice: x: 2, y: 2, z: 4, core: 2. Of those that a mesh axis runs over, the one named last changes fastest.
Arguments:
- panel_rows: bfloat16 [16384, 512], P(('panel', 'col')), may hold values from -6 to 6
- diag_blocks: float32 [512, 512], replicated
- adjoint: bfloat16 [16384, 16384], P('panel', 'col')
- fill: int32 [64, 64], P('panel', 'col'), may hold values from 0 to 1, as said below
Outputs:
- grad_panel: float32 [16384, 512], P(('panel', 'col'))
- grad_diag: float32 [512, 512], replicated
The draws below stay inside these ranges and needn't reach their ends.
Inputs may be any that keep to these rules, and one draw needn't show every extreme that they name: fill is 1 on every diagonal block, fill equals its transpose, and adjoint equals its transpose.
All inputs are finite; a program needn't handle non-finite values.
Results may differ from the reference program's by a relative error of at most 0.004.
Values may be sent and summed in bfloat16 or wider, within the bound.
A program may use at most 128 MiB of HBM per device.

```python
import jax
import jax.numpy as jnp
from jax import lax

B = 256
PW = 512
M = 16384


def draw_diag_blocks(key, part):
    first = jax.random.fold_in(key, 11)
    second = jax.random.fold_in(key, 12)
    amplitude = 2.0 / PW
    noise = jax.random.uniform(first, (PW, PW), jnp.float32, -1.0, 1.0)
    diag = jnp.exp(jax.random.uniform(second, (PW,), jnp.float32, jnp.log(2.5), jnp.log(4.0)))
    off = 0.5 * (noise + noise.T) * amplitude
    eye = (jnp.arange(PW)[:, None] == jnp.arange(PW)[None, :]).astype(jnp.float32)
    return (off * (1.0 - eye) + eye * diag[None, :]).astype(jnp.float32)


def draw_adjoint(key, part):
    first = jax.random.fold_in(key, 21)
    noise = jax.random.normal(first, (M, M), jnp.float32)
    return ((noise + noise.T) * 0.5 ** 0.5 * M ** (-0.5)).astype(jnp.bfloat16)


def draw_fill(key, part):
    first = jax.random.fold_in(key, 31)
    blocks = M // B
    marks = jax.random.randint(first, (blocks, blocks), 0, 4)
    both = jnp.minimum(marks, marks.T) > 0
    eye = jnp.arange(blocks)[:, None] == jnp.arange(blocks)[None, :]
    return jnp.where(eye | both, 1, 0).astype(jnp.int32)


def steps_of(rng, extent, shards, low, top_value):
    def one(dim, shards_of):
        heights = jax.random.uniform(jax.random.fold_in(jax.random.fold_in(rng, 6), dim), (shards_of,), jnp.float32, low / len(shards), top_value / len(shards))
        return jnp.repeat(jnp.exp(heights), extent[dim] // shards_of).reshape((-1,) + (1,) * (len(extent) - dim - 1))

    factor_of = one(*shards[0])
    for cut in shards[1:]:
        factor_of = factor_of * one(*cut)
    return factor_of


def centred(rng, shape, width, most, pieces=(), held_as=jnp.bfloat16):
    entries = jax.random.normal(rng, shape, jnp.float32) * width
    if len(pieces) > 0:
        entries = steps_of(rng, shape, pieces, -0.22, 0.18) * entries
    return jnp.clip(entries, min=-most, max=most).astype(held_as)


def setup_inputs(seed: int = 0) -> dict:
    seeds = jax.random.split(jax.random.key(seed), 5)
    return {
        "panel_rows": centred(seeds[0], (M, PW), 1.0, 6.0, ((0, 32),)),
        "diag_blocks": draw_diag_blocks(jax.random.fold_in(seeds[4], 71), 0),
        "adjoint": draw_adjoint(jax.random.fold_in(seeds[4], 71), 0),
        "fill": draw_fill(jax.random.fold_in(seeds[4], 71), 0),
    }


def factor_with_logdet(matrix):
    lower = jnp.linalg.cholesky(matrix)
    return (lower, 2.0 * jnp.sum(jnp.log(jnp.diagonal(lower))))

def reference(panel_rows, diag_blocks, adjoint, fill):
    lower = jnp.linalg.cholesky(diag_blocks)
    scaled = jax.scipy.linalg.solve_triangular(lower, panel_rows.astype(jnp.float32).T, lower=True).T.astype(jnp.bfloat16)
    blocks = fill.shape[0]

    def block_row(index):
        start = (index * B).astype(jnp.int32)
        rows = lax.dynamic_slice_in_dim(adjoint, start, B, 0)
        marks = lax.dynamic_slice_in_dim(fill, index.astype(jnp.int32), 1, 0)[0].astype(jnp.bfloat16)
        masked = (rows.reshape(B, blocks, B) * marks[None, :, None]).reshape(B, blocks * B)
        return jnp.dot(masked.astype(jnp.float32), scaled.astype(jnp.float32), preferred_element_type=jnp.float32)
    product = lax.map(block_row, jnp.arange(blocks, dtype=jnp.int32)).reshape(blocks * B, PW)
    grad_scaled = -product
    grad_panel = jax.scipy.linalg.solve_triangular(lower, grad_scaled.T, lower=True, trans=1).T
    grad_lower = -jnp.dot(grad_panel.T, scaled.astype(jnp.float32), precision=lax.Precision.HIGHEST)
    grad_lower = jnp.tril(grad_lower)
    outputs, pullback = jax.vjp(factor_with_logdet, diag_blocks)
    grad_diag = pullback((grad_lower, jnp.ones((), jnp.float32)))[0]
    return (grad_panel, grad_diag)
```

```python
import functools

import jax
import jax.numpy as jnp
from jax import lax
from jax.experimental import pallas as pl
from jax.experimental.pallas import tpu as pltpu
from jax.sharding import PartitionSpec as P

B = 256
HIGHEST = lax.Precision.HIGHEST


def inverse_kernel(matrix_ref, out_ref, scaled_ref, x_ref, res_ref):
    n = matrix_ref.shape[0]
    rows = lax.broadcasted_iota(jnp.int32, (n, n), 0)
    cols = lax.broadcasted_iota(jnp.int32, (n, n), 1)
    eye = (rows == cols).astype(jnp.float32)
    matrix = matrix_ref[...]
    only = matrix * eye
    by_row = lax.rsqrt(jnp.sum(only, axis=1, keepdims=True))
    by_col = lax.rsqrt(jnp.sum(only, axis=0, keepdims=True))
    scaled = matrix * by_row * by_col
    scaled_ref[...] = scaled
    bound = jnp.max(jnp.sum(jnp.abs(scaled), axis=1, keepdims=True))
    alpha = jnp.where(bound < 1.9, 1.0, 2.0 / (1.0 + bound))
    x_ref[...] = alpha * (2.0 * eye - alpha * scaled)

    def unfinished(carry):
        step, before, last = carry
        stalled = (last < 0.25) & (last > 0.5 * before)
        return (step < 80) & (last > 1e-6) & jnp.logical_not(stalled)

    def improve(carry):
        step, _, last = carry
        x = x_ref[...]
        res_ref[...] = eye - jnp.dot(
            scaled_ref[...], x, precision=HIGHEST, preferred_element_type=jnp.float32
        )
        res = res_ref[...]
        x_ref[...] = x + jnp.dot(x, res, precision=HIGHEST, preferred_element_type=jnp.float32)
        return step + 1, last, jnp.sum(res * res)

    lax.while_loop(unfinished, improve, (0, jnp.float32(1e30), jnp.float32(1e29)))
    out_ref[...] = x_ref[...] * by_row * by_col


def inverse(matrix):
    n = matrix.shape[0]
    return pl.pallas_call(
        inverse_kernel,
        out_shape=jax.ShapeDtypeStruct((n, n), jnp.float32),
        in_specs=[pl.BlockSpec(memory_space=pltpu.VMEM)],
        out_specs=pl.BlockSpec(memory_space=pltpu.VMEM),
        scratch_shapes=[pltpu.VMEM((n, n), jnp.float32)] * 3,
        compiler_params=pltpu.CompilerParams(vmem_limit_bytes=24 * 1024 * 1024),
        cost_estimate=pl.CostEstimate(
            flops=24 * 2 * n**3, bytes_accessed=8 * n * n, transcendentals=0
        ),
    )(matrix)


def shards(panel_rows, diag_blocks, adjoint, fill):
    n_col = lax.axis_size("col")
    n_pan = lax.axis_size("panel")
    groups = n_pan // n_col
    pairs = []
    for c in range(n_col):
        for k in range(groups):
            for z in range(n_col):
                pairs.append(((groups * c + k) * n_col + z, (k * n_col + z) * n_col + c))
    moved = lax.ppermute(panel_rows, ("panel", "col"), pairs)
    columns = lax.all_gather(moved, "panel", axis=0, tiled=True)
    matrix = 0.5 * (diag_blocks + diag_blocks.T)
    inv = inverse(matrix)
    marks = jnp.repeat(fill, B, axis=0).astype(jnp.bfloat16)
    rows, wide = adjoint.shape
    masked = (adjoint.reshape(rows, wide // B, B) * marks[:, :, None]).reshape(rows, wide)
    partial = jnp.dot(masked, columns, preferred_element_type=jnp.float32)
    product = lax.psum_scatter(
        partial.astype(jnp.bfloat16), "col", scatter_dimension=0, tiled=True
    )
    quad = lax.psum(
        jnp.dot(panel_rows.T, product, preferred_element_type=jnp.float32), ("panel", "col")
    )
    grad_panel = -jnp.dot(product.astype(jnp.float32), inv, precision=lax.Precision.HIGH)
    quad = 0.5 * (quad + quad.T)
    half = jnp.dot(quad, inv, precision=lax.Precision.HIGH)
    grad_diag = inv + 0.5 * jnp.dot(inv, half, precision=lax.Precision.HIGH)
    return (grad_panel, 0.5 * (grad_diag + grad_diag.T))


def solution(mesh):
    in_specs = (P(("panel", "col"), None), P(), P("panel", "col"), P("panel", "col"))
    out_specs = (P(("panel", "col"), None), P())
    return jax.shard_map(shards, mesh=mesh, in_specs=in_specs, out_specs=out_specs, check_vma=False)
```

```python
import functools

import jax
import jax.numpy as jnp
from jax import lax
from jax.experimental import pallas as pl
from jax.experimental.pallas import tpu as pltpu
from jax.sharding import PartitionSpec as P

B = 256
HIGHEST = lax.Precision.HIGHEST


def inverse_kernel(matrix_ref, out_ref, scaled_ref, x_ref, res_ref):
    n = matrix_ref.shape[0]
    rows = lax.broadcasted_iota(jnp.int32, (n, n), 0)
    cols = lax.broadcasted_iota(jnp.int32, (n, n), 1)
    eye = (rows == cols).astype(jnp.float32)
    matrix = matrix_ref[...]
    only = matrix * eye
    by_row = lax.rsqrt(jnp.sum(only, axis=1, keepdims=True))
    by_col = lax.rsqrt(jnp.sum(only, axis=0, keepdims=True))
    scaled = matrix * by_row * by_col
    scaled_ref[...] = scaled
    bound = jnp.max(jnp.sum(jnp.abs(scaled), axis=1, keepdims=True))
    alpha = jnp.where(bound < 1.9, 1.0, 2.0 / (1.0 + bound))
    x_ref[...] = alpha * (2.0 * eye - alpha * scaled)

    def unfinished(carry):
        step, before, last = carry
        stalled = (last < 0.25) & (last > 0.5 * before)
        return (step < 80) & (last > 1e-6) & jnp.logical_not(stalled)

    def improve(carry):
        step, _, last = carry
        x = x_ref[...]
        res_ref[...] = eye - jnp.dot(
            scaled_ref[...], x, precision=HIGHEST, preferred_element_type=jnp.float32
        )
        res = res_ref[...]
        x_ref[...] = x + jnp.dot(x, res, precision=HIGHEST, preferred_element_type=jnp.float32)
        return step + 1, last, jnp.sum(res * res)

    lax.while_loop(unfinished, improve, (0, jnp.float32(1e30), jnp.float32(1e29)))
    out_ref[...] = x_ref[...] * by_row * by_col


def inverse(matrix):
    n = matrix.shape[0]
    return pl.pallas_call(
        inverse_kernel,
        out_shape=jax.ShapeDtypeStruct((n, n), jnp.float32),
        in_specs=[pl.BlockSpec(memory_space=pltpu.VMEM)],
        out_specs=pl.BlockSpec(memory_space=pltpu.VMEM),
        scratch_shapes=[pltpu.VMEM((n, n), jnp.float32)] * 3,
        compiler_params=pltpu.CompilerParams(vmem_limit_bytes=24 * 1024 * 1024),
        cost_estimate=pl.CostEstimate(
            flops=24 * 2 * n**3, bytes_accessed=8 * n * n, transcendentals=0
        ),
    )(matrix)


MESH = pl.DeviceIdType.MESH
F32 = jnp.float32


def greet(peers):
    barrier = pltpu.get_barrier_semaphore()
    for peer in peers:
        pl.semaphore_signal(barrier, inc=1, device_id=peer, device_id_type=MESH)
    pl.semaphore_wait(barrier, len(peers))


def send(src, dst, send_sem, recv_sem, peer):
    copy = pltpu.make_async_remote_copy(
        src_ref=src,
        dst_ref=dst,
        send_sem=send_sem,
        recv_sem=recv_sem,
        device_id=peer,
        device_id_type=MESH,
    )
    copy.start()
    return copy


def collect_kernel(n_pan, block_ref, out_ref, send_sem, recv_sem, fast_send, fast_recv, own_sem):
    me = lax.axis_index("panel")
    chips = n_pan // 2
    chip, core = me // 2, lax.rem(me, 2)
    sibling = {"panel": chip * 2 + 1 - core}
    piece = block_ref.shape[0]
    greet([sibling] + [{"panel": lax.rem(chip + k, chips) * 2 + core} for k in range(1, chips)])

    def place(index):
        return out_ref.at[pl.ds(pl.multiple_of(index * piece, piece), piece)]

    slow = []
    for k in range(1, chips):
        peer = {"panel": lax.rem(chip + k, chips) * 2 + core}
        slow.append(send(block_ref, place(me), send_sem.at[k - 1], recv_sem.at[k - 1], peer))
    fast = [send(block_ref, place(me), fast_send.at[0], fast_recv.at[0], sibling)]
    own = pltpu.make_async_copy(block_ref, place(me), own_sem)
    own.start()
    for k in range(1, chips):
        slow[k - 1].wait_recv()
        held = place(lax.rem(chip + chips - k, chips) * 2 + core)
        fast.append(send(held, held, fast_send.at[k], fast_recv.at[k], sibling))
    own.wait()
    for copy in slow:
        copy.wait_send()
    for copy in fast:
        copy.wait()


def collect(block):
    n_pan = lax.axis_size("panel")
    chips = n_pan // 2
    piece, width = block.shape
    return pl.pallas_call(
        functools.partial(collect_kernel, n_pan),
        out_shape=jax.ShapeDtypeStruct((n_pan * piece, width), block.dtype),
        in_specs=[pl.BlockSpec(memory_space=pl.ANY)],
        out_specs=pl.BlockSpec(memory_space=pl.ANY),
        scratch_shapes=[
            pltpu.SemaphoreType.DMA((chips,)),
            pltpu.SemaphoreType.DMA((chips,)),
            pltpu.SemaphoreType.DMA((chips,)),
            pltpu.SemaphoreType.DMA((chips,)),
            pltpu.SemaphoreType.DMA,
        ],
        compiler_params=pltpu.CompilerParams(collective_id=0, has_side_effects=True),
    )(block)


def multiply_kernel(fill_ref, a_ref, columns_ref, out_ref, total):
    row = pl.program_id(0)
    total[...] = jnp.zeros_like(total)
    for j in range(a_ref.shape[1] // B):

        @pl.when(fill_ref[row, j] != 0)
        def _():
            total[...] += jnp.dot(
                a_ref[:, j * B : (j + 1) * B],
                columns_ref[j * B : (j + 1) * B, :],
                preferred_element_type=F32,
            )

    out_ref[...] = total[...].astype(out_ref.dtype)


def multiply(fill, adjoint, columns):
    rows, wide = adjoint.shape
    width = columns.shape[1]
    return pl.pallas_call(
        multiply_kernel,
        grid=(rows // B,),
        out_shape=jax.ShapeDtypeStruct((rows, width), jnp.bfloat16),
        in_specs=[
            pl.BlockSpec(memory_space=pltpu.SMEM),
            pl.BlockSpec((B, wide), lambda i: (i, 0)),
            pl.BlockSpec((wide, width), lambda i: (0, 0)),
        ],
        out_specs=pl.BlockSpec((B, width), lambda i: (i, 0)),
        scratch_shapes=[pltpu.VMEM((B, width), F32)],
        compiler_params=pltpu.CompilerParams(vmem_limit_bytes=32 * 1024 * 1024),
        cost_estimate=pl.CostEstimate(
            flops=2 * rows * wide * width, bytes_accessed=2 * rows * wide, transcendentals=0
        ),
    )(fill, adjoint, columns)


def halves(x):
    high = x.astype(jnp.bfloat16)
    return high, (x - high.astype(F32)).astype(jnp.bfloat16)


def dot3(x, y):
    (xh, xl), (yh, yl) = halves(x), halves(y)
    mul = functools.partial(jnp.dot, preferred_element_type=F32)
    return mul(xh, yh) + (mul(xh, yl) + mul(xl, yh))


def finish_kernel(
    n_pan, n_col, part_ref, rows_t_ref, inv_ref, panel_ref, diag_ref,
    came, summed, quad, quad_came, slab, stacked, full,
    send0, recv0, send1, recv1, send2, recv2, send3, recv3,
):
    pan, col = lax.axis_index("panel"), lax.axis_index("col")
    pans = [lax.rem(pan + k, n_pan) for k in range(1, n_pan)]
    cols = [lax.rem(col + k, n_col) for k in range(1, n_col)]
    piece = came.shape[1]
    high = slab.shape[0]
    greet([{"panel": p} for p in pans] + [{"col": c} for c in cols])

    copies = []
    for k, c in enumerate(cols):
        src = part_ref.at[pl.ds(pl.multiple_of(c * piece, piece), piece)]
        copies.append(send(src, came.at[k], send0.at[k], recv0.at[k], {"col": c}))
    summed[...] = part_ref[pl.ds(pl.multiple_of(col * piece, piece), piece), :].astype(F32)
    for k in reversed(range(n_col - 1)):
        copies[k].wait_recv()
        summed[...] += came[k].astype(F32)

    sum_high, sum_low = halves(summed[...])
    quad[...] = jnp.dot(rows_t_ref[...], sum_high, preferred_element_type=F32) + jnp.dot(
        rows_t_ref[...], sum_low, preferred_element_type=F32
    )
    for k, p in enumerate(pans):
        src = quad.at[pl.ds(pl.multiple_of(p * high, high), high)]
        copies.append(send(src, quad_came.at[k], send1.at[k], recv1.at[k], {"panel": p}))
    panel_ref[...] = -dot3(summed[...], inv_ref[...])
    mine = quad[pl.ds(pl.multiple_of(pan * high, high), high), :]
    for k in range(n_pan - 1):
        copies[n_col - 1 + k].wait_recv()
        mine = mine + quad_came[k]
    slab[...] = mine
    stacked[col] = mine
    over_col = []
    for k, c in enumerate(cols):
        over_col.append(send(slab, stacked.at[col], send2.at[k], recv2.at[k], {"col": c}))
    for copy in over_col:
        copy.wait()
    total = stacked[0]
    for c in range(1, n_col):
        total = total + stacked[c]
    slab[...] = total
    here = full.at[pl.ds(pl.multiple_of(pan * high, high), high)]
    here[...] = total
    back = []
    for k, p in enumerate(pans):
        back.append(send(slab, here, send3.at[k], recv3.at[k], {"panel": p}))
    for copy in copies:
        copy.wait_send()
    for copy in back:
        copy.wait()
    inv = inv_ref[...]
    grown = dot3(inv, dot3(full[...], inv))
    diag_ref[...] = inv + 0.25 * (grown + grown.T)


def finish(part, rows_t, inv):
    n_pan, n_col = lax.axis_size("panel"), lax.axis_size("col")
    piece = part.shape[0] // n_col
    width = part.shape[1]
    high = width // n_pan
    vmem = pl.BlockSpec(memory_space=pltpu.VMEM)
    dma = pltpu.SemaphoreType.DMA
    return pl.pallas_call(
        functools.partial(finish_kernel, n_pan, n_col),
        out_shape=(
            jax.ShapeDtypeStruct((piece, width), F32),
            jax.ShapeDtypeStruct((width, width), F32),
        ),
        in_specs=[vmem] * 3,
        out_specs=(vmem, vmem),
        scratch_shapes=[
            pltpu.VMEM((n_col - 1, piece, width), jnp.bfloat16),
            pltpu.VMEM((piece, width), F32),
            pltpu.VMEM((width, width), F32),
            pltpu.VMEM((n_pan - 1, high, width), F32),
            pltpu.VMEM((high, width), F32),
            pltpu.VMEM((n_col, high, width), F32),
            pltpu.VMEM((width, width), F32),
            dma((n_col - 1,)), dma((n_col - 1,)),
            dma((n_pan - 1,)), dma((n_pan - 1,)),
            dma((n_col - 1,)), dma((n_col - 1,)),
            dma((n_pan - 1,)), dma((n_pan - 1,)),
        ],
        compiler_params=pltpu.CompilerParams(
            collective_id=1, has_side_effects=True, vmem_limit_bytes=40 * 1024 * 1024
        ),
    )(part, rows_t, inv)


def shards(panel_rows, diag_blocks, adjoint, fill):
    n_col = lax.axis_size("col")
    n_pan = lax.axis_size("panel")
    groups = n_pan // n_col
    pairs = []
    for c in range(n_col):
        for k in range(groups):
            for z in range(n_col):
                pairs.append(((groups * c + k) * n_col + z, (k * n_col + z) * n_col + c))
    moved = lax.ppermute(panel_rows, ("panel", "col"), pairs)
    inv = inverse(0.5 * (diag_blocks + diag_blocks.T))
    part = multiply(fill, adjoint, collect(moved))
    return finish(part, panel_rows.T, inv)


def solution(mesh):
    in_specs = (P(("panel", "col"), None), P(), P("panel", "col"), P("panel", "col"))
    out_specs = (P(("panel", "col"), None), P())
    return jax.shard_map(shards, mesh=mesh, in_specs=in_specs, out_specs=out_specs, check_vma=False)
```

```python
import functools

import jax
import jax.numpy as jnp
from jax import lax
from jax.experimental import pallas as pl
from jax.experimental.pallas import tpu as pltpu
from jax.sharding import PartitionSpec as P

B = 256
HIGHEST = lax.Precision.HIGHEST


def inverse_kernel(matrix_ref, out_ref, scaled_ref, x_ref, res_ref):
    n = matrix_ref.shape[0]
    rows = lax.broadcasted_iota(jnp.int32, (n, n), 0)
    cols = lax.broadcasted_iota(jnp.int32, (n, n), 1)
    eye = (rows == cols).astype(jnp.float32)
    matrix = matrix_ref[...]
    only = matrix * eye
    by_row = lax.rsqrt(jnp.sum(only, axis=1, keepdims=True))
    by_col = lax.rsqrt(jnp.sum(only, axis=0, keepdims=True))
    scaled = matrix * by_row * by_col
    scaled_ref[...] = scaled
    bound = jnp.max(jnp.sum(jnp.abs(scaled), axis=1, keepdims=True))
    alpha = jnp.where(bound < 1.9, 1.0, 2.0 / (1.0 + bound))
    x_ref[...] = alpha * (2.0 * eye - alpha * scaled)

    def unfinished(carry):
        step, before, last = carry
        stalled = (last < 0.25) & (last > 0.5 * before)
        return (step < 80) & (last > 1e-6) & jnp.logical_not(stalled)

    def improve(carry):
        step, _, last = carry
        x = x_ref[...]
        res_ref[...] = eye - jnp.dot(
            scaled_ref[...], x, precision=HIGHEST, preferred_element_type=jnp.float32
        )
        res = res_ref[...]
        x_ref[...] = x + jnp.dot(x, res, precision=HIGHEST, preferred_element_type=jnp.float32)
        return step + 1, last, jnp.sum(res * res)

    lax.while_loop(unfinished, improve, (0, jnp.float32(1e30), jnp.float32(1e29)))
    out_ref[...] = x_ref[...] * by_row * by_col


def inverse(matrix):
    n = matrix.shape[0]
    return pl.pallas_call(
        inverse_kernel,
        out_shape=jax.ShapeDtypeStruct((n, n), jnp.float32),
        in_specs=[pl.BlockSpec(memory_space=pltpu.VMEM)],
        out_specs=pl.BlockSpec(memory_space=pltpu.VMEM),
        scratch_shapes=[pltpu.VMEM((n, n), jnp.float32)] * 3,
        compiler_params=pltpu.CompilerParams(vmem_limit_bytes=24 * 1024 * 1024),
        cost_estimate=pl.CostEstimate(
            flops=24 * 2 * n**3, bytes_accessed=8 * n * n, transcendentals=0
        ),
    )(matrix)


MESH = pl.DeviceIdType.MESH
F32 = jnp.float32


def greet(peers):
    barrier = pltpu.get_barrier_semaphore()
    for peer in peers:
        pl.semaphore_signal(barrier, inc=1, device_id=peer, device_id_type=MESH)
    pl.semaphore_wait(barrier, len(peers))


def send(src, dst, send_sem, recv_sem, peer):
    copy = pltpu.make_async_remote_copy(
        src_ref=src,
        dst_ref=dst,
        send_sem=send_sem,
        recv_sem=recv_sem,
        device_id=peer,
        device_id_type=MESH,
    )
    copy.start()
    return copy


def collect_kernel(n_pan, block_ref, out_ref, send_sem, recv_sem, fast_send, fast_recv, own_sem):
    me = lax.axis_index("panel")
    chips = n_pan // 2
    chip, core = me // 2, lax.rem(me, 2)
    sibling = {"panel": chip * 2 + 1 - core}
    piece = block_ref.shape[0]
    greet([sibling] + [{"panel": lax.rem(chip + k, chips) * 2 + core} for k in range(1, chips)])

    def place(index):
        return out_ref.at[pl.ds(pl.multiple_of(index * piece, piece), piece)]

    slow = []
    for k in range(1, chips):
        peer = {"panel": lax.rem(chip + k, chips) * 2 + core}
        slow.append(send(block_ref, place(me), send_sem.at[k - 1], recv_sem.at[k - 1], peer))
    fast = [send(block_ref, place(me), fast_send.at[0], fast_recv.at[0], sibling)]
    own = pltpu.make_async_copy(block_ref, place(me), own_sem)
    own.start()
    for k in range(1, chips):
        slow[k - 1].wait_recv()
        held = place(lax.rem(chip + chips - k, chips) * 2 + core)
        fast.append(send(held, held, fast_send.at[k], fast_recv.at[k], sibling))
    own.wait()
    for copy in slow:
        copy.wait_send()
    for copy in fast:
        copy.wait()


def collect(block):
    n_pan = lax.axis_size("panel")
    chips = n_pan // 2
    piece, width = block.shape
    return pl.pallas_call(
        functools.partial(collect_kernel, n_pan),
        out_shape=jax.ShapeDtypeStruct((n_pan * piece, width), block.dtype),
        in_specs=[pl.BlockSpec(memory_space=pl.ANY)],
        out_specs=pl.BlockSpec(memory_space=pl.ANY),
        scratch_shapes=[
            pltpu.SemaphoreType.DMA((chips,)),
            pltpu.SemaphoreType.DMA((chips,)),
            pltpu.SemaphoreType.DMA((chips,)),
            pltpu.SemaphoreType.DMA((chips,)),
            pltpu.SemaphoreType.DMA,
        ],
        compiler_params=pltpu.CompilerParams(collective_id=0, has_side_effects=True),
    )(block)


def multiply_kernel(start_ref, fill_ref, a_ref, columns_ref, out_ref, total):
    row = start_ref[0] + pl.program_id(0)
    total[...] = jnp.zeros_like(total)
    for j in range(a_ref.shape[1] // B):

        @pl.when(fill_ref[row, j] != 0)
        def _():
            total[...] += jnp.dot(
                a_ref[:, j * B : (j + 1) * B],
                columns_ref[j * B : (j + 1) * B, :],
                preferred_element_type=F32,
            )

    out_ref[...] = total[...].astype(out_ref.dtype)


def multiply(start, rows, fill, adjoint, columns):
    wide, width = columns.shape
    return pl.pallas_call(
        multiply_kernel,
        grid_spec=pltpu.PrefetchScalarGridSpec(
            num_scalar_prefetch=2,
            grid=(rows // B,),
            in_specs=[
                pl.BlockSpec((B, wide), lambda i, s, f: (s[0] + i, 0)),
                pl.BlockSpec((wide, width), lambda i, s, f: (0, 0)),
            ],
            out_specs=pl.BlockSpec((B, width), lambda i, s, f: (i, 0)),
            scratch_shapes=[pltpu.VMEM((B, width), F32)],
        ),
        out_shape=jax.ShapeDtypeStruct((rows, width), jnp.bfloat16),
        compiler_params=pltpu.CompilerParams(vmem_limit_bytes=32 * 1024 * 1024),
        cost_estimate=pl.CostEstimate(
            flops=2 * rows * wide * width, bytes_accessed=2 * rows * wide, transcendentals=0
        ),
    )(start, fill, adjoint, columns)


def halves(x):
    high = x.astype(jnp.bfloat16)
    return high, (x - high.astype(F32)).astype(jnp.bfloat16)


def dot3(x, y):
    (xh, xl), (yh, yl) = halves(x), halves(y)
    mul = functools.partial(jnp.dot, preferred_element_type=F32)
    return mul(xh, yh) + (mul(xh, yl) + mul(xl, yh))


def finish_kernel(
    n_pan, n_col, *refs
):
    parts, refs = refs[:n_col], refs[n_col:]
    rows_t_ref, inv_ref, panel_ref, diag_ref, *refs = refs
    summed, quad, quad_came, slab, stacked, full, *refs = refs
    send1, recv1, send2, recv2, send3, recv3 = refs
    pan, col = lax.axis_index("panel"), lax.axis_index("col")
    pans = [lax.rem(pan + k, n_pan) for k in range(1, n_pan)]
    cols = [lax.rem(col + k, n_col) for k in range(1, n_col)]
    high = slab.shape[0]
    greet([{"panel": p} for p in pans] + [{"col": c} for c in cols])

    copies = []
    total = parts[0][...].astype(F32)
    for part in parts[1:]:
        total = total + part[...].astype(F32)
    summed[...] = total

    sum_high, sum_low = halves(summed[...])
    quad[...] = jnp.dot(rows_t_ref[...], sum_high, preferred_element_type=F32) + jnp.dot(
        rows_t_ref[...], sum_low, preferred_element_type=F32
    )
    for k, p in enumerate(pans):
        src = quad.at[pl.ds(pl.multiple_of(p * high, high), high)]
        copies.append(send(src, quad_came.at[k], send1.at[k], recv1.at[k], {"panel": p}))
    panel_ref[...] = -dot3(summed[...], inv_ref[...])
    mine = quad[pl.ds(pl.multiple_of(pan * high, high), high), :]
    for k in range(n_pan - 1):
        copies[k].wait_recv()
        mine = mine + quad_came[k]
    slab[...] = mine
    stacked[col] = mine
    over_col = []
    for k, c in enumerate(cols):
        over_col.append(send(slab, stacked.at[col], send2.at[k], recv2.at[k], {"col": c}))
    for copy in over_col:
        copy.wait()
    total = stacked[0]
    for c in range(1, n_col):
        total = total + stacked[c]
    slab[...] = total
    here = full.at[pl.ds(pl.multiple_of(pan * high, high), high)]
    here[...] = total
    back = []
    for k, p in enumerate(pans):
        back.append(send(slab, here, send3.at[k], recv3.at[k], {"panel": p}))
    for copy in copies:
        copy.wait_send()
    for copy in back:
        copy.wait()
    inv = inv_ref[...]
    grown = dot3(inv, dot3(full[...], inv))
    diag_ref[...] = inv + 0.25 * (grown + grown.T)


def finish(parts, rows_t, inv):
    n_pan, n_col = lax.axis_size("panel"), lax.axis_size("col")
    piece, width = parts[0].shape
    high = width // n_pan
    vmem = pl.BlockSpec(memory_space=pltpu.VMEM)
    dma = pltpu.SemaphoreType.DMA
    return pl.pallas_call(
        functools.partial(finish_kernel, n_pan, n_col),
        out_shape=(
            jax.ShapeDtypeStruct((piece, width), F32),
            jax.ShapeDtypeStruct((width, width), F32),
        ),
        in_specs=[vmem] * (n_col + 2),
        out_specs=(vmem, vmem),
        scratch_shapes=[
            pltpu.VMEM((piece, width), F32),
            pltpu.VMEM((width, width), F32),
            pltpu.VMEM((n_pan - 1, high, width), F32),
            pltpu.VMEM((high, width), F32),
            pltpu.VMEM((n_col, high, width), F32),
            pltpu.VMEM((width, width), F32),
            dma((n_pan - 1,)), dma((n_pan - 1,)),
            dma((n_col - 1,)), dma((n_col - 1,)),
            dma((n_pan - 1,)), dma((n_pan - 1,)),
        ],
        compiler_params=pltpu.CompilerParams(
            collective_id=1, has_side_effects=True, vmem_limit_bytes=40 * 1024 * 1024
        ),
    )(*parts, rows_t, inv)


def shards(panel_rows, diag_blocks, adjoint, fill):
    n_col = lax.axis_size("col")
    n_pan = lax.axis_size("panel")
    groups = n_pan // n_col
    pairs = []
    for c in range(n_col):
        for k in range(groups):
            for z in range(n_col):
                pairs.append(((groups * c + k) * n_col + z, (k * n_col + z) * n_col + c))
    moved = lax.ppermute(panel_rows, ("panel", "col"), pairs)
    inv = inverse(0.5 * (diag_blocks + diag_blocks.T))
    columns = collect(moved)
    piece = panel_rows.shape[0]
    col = lax.axis_index("col")
    parts = []
    for k in range(n_col - 1, -1, -1):
        start = lax.rem(col + k, n_col) * (piece // B)
        part = multiply(start.astype(jnp.int32)[None], piece, fill, adjoint, columns)
        if k:
            part = lax.ppermute(part, "col", [(c, (c + k) % n_col) for c in range(n_col)])
        parts.append(part)
    return finish(parts, panel_rows.T, inv)


def solution(mesh):
    in_specs = (P(("panel", "col"), None), P(), P("panel", "col"), P("panel", "col"))
    out_specs = (P(("panel", "col"), None), P())
    return jax.shard_map(shards, mesh=mesh, in_specs=in_specs, out_specs=out_specs, check_vma=False)
```

```python
import functools

import jax
import jax.numpy as jnp
from jax import lax
from jax.experimental import pallas as pl
from jax.experimental.pallas import tpu as pltpu
from jax.sharding import PartitionSpec as P

B = 256
HIGHEST = lax.Precision.HIGHEST


def inverse_kernel(matrix_ref, out_ref, scaled_ref, x_ref, res_ref):
    n = matrix_ref.shape[0]
    rows = lax.broadcasted_iota(jnp.int32, (n, n), 0)
    cols = lax.broadcasted_iota(jnp.int32, (n, n), 1)
    eye = (rows == cols).astype(jnp.float32)
    matrix = matrix_ref[...]
    only = matrix * eye
    by_row = lax.rsqrt(jnp.sum(only, axis=1, keepdims=True))
    by_col = lax.rsqrt(jnp.sum(only, axis=0, keepdims=True))
    scaled = matrix * by_row * by_col
    scaled_ref[...] = scaled
    bound = jnp.max(jnp.sum(jnp.abs(scaled), axis=1, keepdims=True))
    alpha = jnp.where(bound < 1.9, 1.0, 2.0 / (1.0 + bound))
    x_ref[...] = alpha * (2.0 * eye - alpha * scaled)

    def unfinished(carry):
        step, before, last = carry
        stalled = (last < 0.25) & (last > 0.5 * before)
        return (step < 80) & (last > 1e-6) & jnp.logical_not(stalled)

    def improve(carry):
        step, _, last = carry
        x = x_ref[...]
        res_ref[...] = eye - jnp.dot(
            scaled_ref[...], x, precision=HIGHEST, preferred_element_type=jnp.float32
        )
        res = res_ref[...]
        x_ref[...] = x + jnp.dot(x, res, precision=HIGHEST, preferred_element_type=jnp.float32)
        return step + 1, last, jnp.sum(res * res)

    lax.while_loop(unfinished, improve, (0, jnp.float32(1e30), jnp.float32(1e29)))
    out_ref[...] = x_ref[...] * by_row * by_col


def inverse(matrix):
    n = matrix.shape[0]
    return pl.pallas_call(
        inverse_kernel,
        out_shape=jax.ShapeDtypeStruct((n, n), jnp.float32),
        in_specs=[pl.BlockSpec(memory_space=pltpu.VMEM)],
        out_specs=pl.BlockSpec(memory_space=pltpu.VMEM),
        scratch_shapes=[pltpu.VMEM((n, n), jnp.float32)] * 3,
        compiler_params=pltpu.CompilerParams(vmem_limit_bytes=24 * 1024 * 1024),
        cost_estimate=pl.CostEstimate(
            flops=24 * 2 * n**3, bytes_accessed=8 * n * n, transcendentals=0
        ),
    )(matrix)


MESH = pl.DeviceIdType.MESH
F32 = jnp.float32


def greet(peers):
    barrier = pltpu.get_barrier_semaphore()
    for peer in peers:
        pl.semaphore_signal(barrier, inc=1, device_id=peer, device_id_type=MESH)
    pl.semaphore_wait(barrier, len(peers))


def send(src, dst, send_sem, recv_sem, peer):
    copy = pltpu.make_async_remote_copy(
        src_ref=src,
        dst_ref=dst,
        send_sem=send_sem,
        recv_sem=recv_sem,
        device_id=peer,
        device_id_type=MESH,
    )
    copy.start()
    return copy


def collect_kernel(n_pan, block_ref, out_ref, send_sem, recv_sem, fast_send, fast_recv, own_sem):
    me = lax.axis_index("panel")
    chips = n_pan // 2
    chip, core = me // 2, lax.rem(me, 2)
    sibling = {"panel": chip * 2 + 1 - core}
    piece = block_ref.shape[0]
    greet([sibling] + [{"panel": lax.rem(chip + k, chips) * 2 + core} for k in range(1, chips)])

    def place(index):
        return out_ref.at[pl.ds(pl.multiple_of(index * piece, piece), piece)]

    slow = []
    for k in range(1, chips):
        peer = {"panel": lax.rem(chip + k, chips) * 2 + core}
        slow.append(send(block_ref, place(me), send_sem.at[k - 1], recv_sem.at[k - 1], peer))
    fast = [send(block_ref, place(me), fast_send.at[0], fast_recv.at[0], sibling)]
    own = pltpu.make_async_copy(block_ref, place(me), own_sem)
    own.start()
    for k in range(1, chips):
        slow[k - 1].wait_recv()
        held = place(lax.rem(chip + chips - k, chips) * 2 + core)
        fast.append(send(held, held, fast_send.at[k], fast_recv.at[k], sibling))
    own.wait()
    for copy in slow:
        copy.wait_send()
    for copy in fast:
        copy.wait()


def collect(block):
    n_pan = lax.axis_size("panel")
    chips = n_pan // 2
    piece, width = block.shape
    return pl.pallas_call(
        functools.partial(collect_kernel, n_pan),
        out_shape=jax.ShapeDtypeStruct((n_pan * piece, width), block.dtype),
        in_specs=[pl.BlockSpec(memory_space=pl.ANY)],
        out_specs=pl.BlockSpec(memory_space=pl.ANY),
        scratch_shapes=[
            pltpu.SemaphoreType.DMA((chips,)),
            pltpu.SemaphoreType.DMA((chips,)),
            pltpu.SemaphoreType.DMA((chips,)),
            pltpu.SemaphoreType.DMA((chips,)),
            pltpu.SemaphoreType.DMA,
        ],
        compiler_params=pltpu.CompilerParams(collective_id=0, has_side_effects=True),
    )(block)


def multiply_kernel(start_ref, fill_ref, a_ref, columns_ref, out_ref, total):
    row = start_ref[0] + pl.program_id(0)
    total[...] = jnp.zeros_like(total)
    for j in range(a_ref.shape[1] // B):

        @pl.when(fill_ref[row, j] != 0)
        def _():
            total[...] += jnp.dot(
                a_ref[:, j * B : (j + 1) * B],
                columns_ref[j * B : (j + 1) * B, :],
                preferred_element_type=F32,
            )

    out_ref[...] = total[...].astype(out_ref.dtype)


def multiply(start, rows, fill, adjoint, columns):
    wide, width = columns.shape
    return pl.pallas_call(
        multiply_kernel,
        grid_spec=pltpu.PrefetchScalarGridSpec(
            num_scalar_prefetch=2,
            grid=(rows // B,),
            in_specs=[
                pl.BlockSpec((B, wide), lambda i, s, f: (s[0] + i, 0)),
                pl.BlockSpec((wide, width), lambda i, s, f: (0, 0)),
            ],
            out_specs=pl.BlockSpec((B, width), lambda i, s, f: (i, 0)),
            scratch_shapes=[pltpu.VMEM((B, width), F32)],
        ),
        out_shape=jax.ShapeDtypeStruct((rows, width), jnp.bfloat16),
        compiler_params=pltpu.CompilerParams(vmem_limit_bytes=56 * 1024 * 1024),
        cost_estimate=pl.CostEstimate(
            flops=2 * rows * wide * width, bytes_accessed=2 * rows * wide, transcendentals=0
        ),
    )(start, fill, adjoint, columns)


def halves(x):
    high = x.astype(jnp.bfloat16)
    return high, (x - high.astype(F32)).astype(jnp.bfloat16)


def dot3(x, y):
    (xh, xl), (yh, yl) = halves(x), halves(y)
    mul = functools.partial(jnp.dot, preferred_element_type=F32)
    return mul(xh, yh) + (mul(xh, yl) + mul(xl, yh))


def finish_kernel(
    n_pan, n_col, *refs
):
    parts, refs = refs[:n_col], refs[n_col:]
    rows_t_ref, inv_ref, panel_ref, diag_ref, *refs = refs
    summed, quad, quad_came, slab, stacked, full, *refs = refs
    send1, recv1, send2, recv2, send3, recv3 = refs
    pan, col = lax.axis_index("panel"), lax.axis_index("col")
    pans = [lax.rem(pan + k, n_pan) for k in range(1, n_pan)]
    cols = [lax.rem(col + k, n_col) for k in range(1, n_col)]
    high = slab.shape[0]
    greet([{"panel": p} for p in pans] + [{"col": c} for c in cols])

    copies = []
    total = parts[0][...].astype(F32)
    for part in parts[1:]:
        total = total + part[...].astype(F32)
    summed[...] = total

    sum_high, sum_low = halves(summed[...])
    quad[...] = jnp.dot(rows_t_ref[...], sum_high, preferred_element_type=F32) + jnp.dot(
        rows_t_ref[...], sum_low, preferred_element_type=F32
    )
    for k, p in enumerate(pans):
        src = quad.at[pl.ds(pl.multiple_of(p * high, high), high)]
        copies.append(send(src, quad_came.at[k], send1.at[k], recv1.at[k], {"panel": p}))
    panel_ref[...] = -dot3(summed[...], inv_ref[...])
    mine = quad[pl.ds(pl.multiple_of(pan * high, high), high), :]
    for k in range(n_pan - 1):
        copies[k].wait_recv()
        mine = mine + quad_came[k]
    slab[...] = mine
    stacked[col] = mine
    over_col = []
    for k, c in enumerate(cols):
        over_col.append(send(slab, stacked.at[col], send2.at[k], recv2.at[k], {"col": c}))
    for copy in over_col:
        copy.wait()
    total = stacked[0]
    for c in range(1, n_col):
        total = total + stacked[c]
    slab[...] = total
    here = full.at[pl.ds(pl.multiple_of(pan * high, high), high)]
    here[...] = total
    back = []
    for k, p in enumerate(pans):
        back.append(send(slab, here, send3.at[k], recv3.at[k], {"panel": p}))
    for copy in copies:
        copy.wait_send()
    for copy in back:
        copy.wait()
    inv = inv_ref[...]
    grown = dot3(inv, dot3(full[...], inv))
    diag_ref[...] = inv + 0.25 * (grown + grown.T)


def finish(parts, rows_t, inv):
    n_pan, n_col = lax.axis_size("panel"), lax.axis_size("col")
    piece, width = parts[0].shape
    high = width // n_pan
    vmem = pl.BlockSpec(memory_space=pltpu.VMEM)
    dma = pltpu.SemaphoreType.DMA
    return pl.pallas_call(
        functools.partial(finish_kernel, n_pan, n_col),
        out_shape=(
            jax.ShapeDtypeStruct((piece, width), F32),
            jax.ShapeDtypeStruct((width, width), F32),
        ),
        in_specs=[vmem] * (n_col + 2),
        out_specs=(vmem, vmem),
        scratch_shapes=[
            pltpu.VMEM((piece, width), F32),
            pltpu.VMEM((width, width), F32),
            pltpu.VMEM((n_pan - 1, high, width), F32),
            pltpu.VMEM((high, width), F32),
            pltpu.VMEM((n_col, high, width), F32),
            pltpu.VMEM((width, width), F32),
            dma((n_pan - 1,)), dma((n_pan - 1,)),
            dma((n_col - 1,)), dma((n_col - 1,)),
            dma((n_pan - 1,)), dma((n_pan - 1,)),
        ],
        compiler_params=pltpu.CompilerParams(
            collective_id=1, has_side_effects=True, vmem_limit_bytes=40 * 1024 * 1024
        ),
    )(*parts, rows_t, inv)


def shards(panel_rows, diag_blocks, adjoint, fill):
    n_col = lax.axis_size("col")
    n_pan = lax.axis_size("panel")
    groups = n_pan // n_col
    pairs = []
    for c in range(n_col):
        for k in range(groups):
            for z in range(n_col):
                pairs.append(((groups * c + k) * n_col + z, (k * n_col + z) * n_col + c))
    moved = lax.ppermute(panel_rows, ("panel", "col"), pairs)
    inv = inverse(0.5 * (diag_blocks + diag_blocks.T))
    columns = collect(moved)
    piece = panel_rows.shape[0]
    col = lax.axis_index("col")
    parts = []
    for k in range(n_col - 1, -1, -1):
        start = lax.rem(col + k, n_col) * (piece // B)
        part = multiply(start.astype(jnp.int32)[None], piece, fill, adjoint, columns)
        if k:
            part = lax.ppermute(part, "col", [(c, (c + k) % n_col) for c in range(n_col)])
        parts.append(part)
    return finish(parts, panel_rows.T, inv)


def solution(mesh):
    in_specs = (P(("panel", "col"), None), P(), P("panel", "col"), P("panel", "col"))
    out_specs = (P(("panel", "col"), None), P())
    return jax.shard_map(shards, mesh=mesh, in_specs=in_specs, out_specs=out_specs, check_vma=False)
```

```python
import functools

import jax
import jax.numpy as jnp
from jax import lax
from jax.experimental import pallas as pl
from jax.experimental.pallas import tpu as pltpu
from jax.sharding import PartitionSpec as P

B = 256
HIGHEST = lax.Precision.HIGHEST


def inverse_kernel(matrix_ref, out_ref, scaled_ref, x_ref, res_ref):
    n = matrix_ref.shape[0]
    rows = lax.broadcasted_iota(jnp.int32, (n, n), 0)
    cols = lax.broadcasted_iota(jnp.int32, (n, n), 1)
    eye = (rows == cols).astype(jnp.float32)
    matrix = matrix_ref[...]
    only = matrix * eye
    by_row = lax.rsqrt(jnp.sum(only, axis=1, keepdims=True))
    by_col = lax.rsqrt(jnp.sum(only, axis=0, keepdims=True))
    scaled = matrix * by_row * by_col
    scaled_ref[...] = scaled
    bound = jnp.max(jnp.sum(jnp.abs(scaled), axis=1, keepdims=True))
    alpha = jnp.where(bound < 1.9, 1.0, 2.0 / (1.0 + bound))
    x_ref[...] = alpha * (2.0 * eye - alpha * scaled)

    def unfinished(carry):
        step, before, last = carry
        stalled = (last < 0.25) & (last > 0.5 * before)
        return (step < 80) & (last > 1e-6) & jnp.logical_not(stalled)

    def improve(carry):
        step, _, last = carry
        x = x_ref[...]
        res_ref[...] = eye - jnp.dot(
            scaled_ref[...], x, precision=HIGHEST, preferred_element_type=jnp.float32
        )
        res = res_ref[...]
        x_ref[...] = x + jnp.dot(x, res, precision=HIGHEST, preferred_element_type=jnp.float32)
        return step + 1, last, jnp.sum(res * res)

    lax.while_loop(unfinished, improve, (0, jnp.float32(1e30), jnp.float32(1e29)))
    out_ref[...] = x_ref[...] * by_row * by_col


def inverse(matrix):
    n = matrix.shape[0]
    return pl.pallas_call(
        inverse_kernel,
        out_shape=jax.ShapeDtypeStruct((n, n), jnp.float32),
        in_specs=[pl.BlockSpec(memory_space=pltpu.VMEM)],
        out_specs=pl.BlockSpec(memory_space=pltpu.VMEM),
        scratch_shapes=[pltpu.VMEM((n, n), jnp.float32)] * 3,
        compiler_params=pltpu.CompilerParams(vmem_limit_bytes=24 * 1024 * 1024),
        cost_estimate=pl.CostEstimate(
            flops=24 * 2 * n**3, bytes_accessed=8 * n * n, transcendentals=0
        ),
    )(matrix)


MESH = pl.DeviceIdType.MESH
F32 = jnp.float32


def greet(peers):
    barrier = pltpu.get_barrier_semaphore()
    for peer in peers:
        pl.semaphore_signal(barrier, inc=1, device_id=peer, device_id_type=MESH)
    pl.semaphore_wait(barrier, len(peers))


def send(src, dst, send_sem, recv_sem, peer):
    copy = pltpu.make_async_remote_copy(
        src_ref=src,
        dst_ref=dst,
        send_sem=send_sem,
        recv_sem=recv_sem,
        device_id=peer,
        device_id_type=MESH,
    )
    copy.start()
    return copy


def collect_kernel(n_pan, block_ref, out_ref, send_sem, recv_sem, fast_send, fast_recv, own_sem):
    me = lax.axis_index("panel")
    chips = n_pan // 2
    chip, core = me // 2, lax.rem(me, 2)
    sibling = {"panel": chip * 2 + 1 - core}
    piece = block_ref.shape[0]
    greet([sibling] + [{"panel": lax.rem(chip + k, chips) * 2 + core} for k in range(1, chips)])

    def place(index):
        return out_ref.at[pl.ds(pl.multiple_of(index * piece, piece), piece)]

    slow = []
    for k in range(1, chips):
        peer = {"panel": lax.rem(chip + k, chips) * 2 + core}
        slow.append(send(block_ref, place(me), send_sem.at[k - 1], recv_sem.at[k - 1], peer))
    fast = [send(block_ref, place(me), fast_send.at[0], fast_recv.at[0], sibling)]
    own = pltpu.make_async_copy(block_ref, place(me), own_sem)
    own.start()
    for k in range(1, chips):
        slow[k - 1].wait_recv()
        held = place(lax.rem(chip + chips - k, chips) * 2 + core)
        fast.append(send(held, held, fast_send.at[k], fast_recv.at[k], sibling))
    own.wait()
    for copy in slow:
        copy.wait_send()
    for copy in fast:
        copy.wait()


def collect(block):
    n_pan = lax.axis_size("panel")
    chips = n_pan // 2
    piece, width = block.shape
    return pl.pallas_call(
        functools.partial(collect_kernel, n_pan),
        out_shape=jax.ShapeDtypeStruct((n_pan * piece, width), block.dtype),
        in_specs=[pl.BlockSpec(memory_space=pl.ANY)],
        out_specs=pl.BlockSpec(memory_space=pl.ANY),
        scratch_shapes=[
            pltpu.SemaphoreType.DMA((chips,)),
            pltpu.SemaphoreType.DMA((chips,)),
            pltpu.SemaphoreType.DMA((chips,)),
            pltpu.SemaphoreType.DMA((chips,)),
            pltpu.SemaphoreType.DMA,
        ],
        compiler_params=pltpu.CompilerParams(collective_id=0, has_side_effects=True),
    )(block)


def multiply_kernel(start_ref, fill_ref, a_ref, columns_ref, out_ref, total):
    row = start_ref[0] + pl.program_id(0)
    total[...] = jnp.zeros_like(total)
    for j in range(a_ref.shape[1] // B):

        @pl.when(fill_ref[row, j] != 0)
        def _():
            total[...] += jnp.dot(
                a_ref[:, j * B : (j + 1) * B],
                columns_ref[j * B : (j + 1) * B, :],
                preferred_element_type=F32,
            )

    out_ref[...] = total[...].astype(out_ref.dtype)


def multiply(start, rows, fill, adjoint, columns):
    wide, width = columns.shape
    return pl.pallas_call(
        multiply_kernel,
        grid_spec=pltpu.PrefetchScalarGridSpec(
            num_scalar_prefetch=2,
            grid=(rows // B,),
            in_specs=[
                pl.BlockSpec((B, wide), lambda i, s, f: (s[0] + i, 0)),
                pl.BlockSpec((wide, width), lambda i, s, f: (0, 0)),
            ],
            out_specs=pl.BlockSpec((B, width), lambda i, s, f: (i, 0)),
            scratch_shapes=[pltpu.VMEM((B, width), F32)],
        ),
        out_shape=jax.ShapeDtypeStruct((rows, width), jnp.bfloat16),
        compiler_params=pltpu.CompilerParams(vmem_limit_bytes=56 * 1024 * 1024),
        cost_estimate=pl.CostEstimate(
            flops=2 * rows * wide * width, bytes_accessed=2 * rows * wide, transcendentals=0
        ),
    )(start, fill, adjoint, columns)


def halves(x):
    high = x.astype(jnp.bfloat16)
    return high, (x - high.astype(F32)).astype(jnp.bfloat16)


def dot3(x, y):
    (xh, xl), (yh, yl) = halves(x), halves(y)
    mul = functools.partial(jnp.dot, preferred_element_type=F32)
    return mul(xh, yh) + (mul(xh, yl) + mul(xl, yh))


def finish_kernel(
    n_pan, n_col, *refs
):
    parts, refs = refs[:n_col], refs[n_col:]
    rows_t_ref, inv_ref, panel_ref, diag_ref, *refs = refs
    summed, quad, quad_came, slab, stacked, full, *refs = refs
    send1, recv1, send2, recv2, send3, recv3 = refs
    pan, col = lax.axis_index("panel"), lax.axis_index("col")
    pans = [lax.rem(pan + k, n_pan) for k in range(1, n_pan)]
    cols = [lax.rem(col + k, n_col) for k in range(1, n_col)]
    high = slab.shape[0]
    greet([{"panel": p} for p in pans] + [{"col": c} for c in cols])

    copies = []
    total = parts[0][...].astype(F32)
    for part in parts[1:]:
        total = total + part[...].astype(F32)
    summed[...] = total

    sum_high, sum_low = halves(summed[...])
    own = jnp.dot(rows_t_ref[...], sum_high, preferred_element_type=F32) + jnp.dot(
        rows_t_ref[...], sum_low, preferred_element_type=F32
    )
    quad[...] = own.astype(quad.dtype)
    for k, p in enumerate(pans):
        src = quad.at[pl.ds(pl.multiple_of(p * high, high), high)]
        copies.append(send(src, quad_came.at[k], send1.at[k], recv1.at[k], {"panel": p}))
    panel_ref[...] = -dot3(summed[...], inv_ref[...])
    mine = quad[pl.ds(pl.multiple_of(pan * high, high), high), :].astype(F32)
    for k in range(n_pan - 1):
        copies[k].wait_recv()
        mine = mine + quad_came[k].astype(F32)
    slab[...] = mine
    stacked[col] = mine
    over_col = []
    for k, c in enumerate(cols):
        over_col.append(send(slab, stacked.at[col], send2.at[k], recv2.at[k], {"col": c}))
    for copy in over_col:
        copy.wait()
    total = stacked[0]
    for c in range(1, n_col):
        total = total + stacked[c]
    slab[...] = total
    here = full.at[pl.ds(pl.multiple_of(pan * high, high), high)]
    here[...] = total
    back = []
    for k, p in enumerate(pans):
        back.append(send(slab, here, send3.at[k], recv3.at[k], {"panel": p}))
    for copy in copies:
        copy.wait_send()
    for copy in back:
        copy.wait()
    inv = inv_ref[...]
    grown = dot3(inv, dot3(full[...], inv))
    diag_ref[...] = inv + 0.25 * (grown + grown.T)


def finish(parts, rows_t, inv):
    n_pan, n_col = lax.axis_size("panel"), lax.axis_size("col")
    piece, width = parts[0].shape
    high = width // n_pan
    vmem = pl.BlockSpec(memory_space=pltpu.VMEM)
    dma = pltpu.SemaphoreType.DMA
    return pl.pallas_call(
        functools.partial(finish_kernel, n_pan, n_col),
        out_shape=(
            jax.ShapeDtypeStruct((piece, width), F32),
            jax.ShapeDtypeStruct((width, width), F32),
        ),
        in_specs=[vmem] * (n_col + 2),
        out_specs=(vmem, vmem),
        scratch_shapes=[
            pltpu.VMEM((piece, width), F32),
            pltpu.VMEM((width, width), jnp.bfloat16),
            pltpu.VMEM((n_pan - 1, high, width), jnp.bfloat16),
            pltpu.VMEM((high, width), F32),
            pltpu.VMEM((n_col, high, width), F32),
            pltpu.VMEM((width, width), F32),
            dma((n_pan - 1,)), dma((n_pan - 1,)),
            dma((n_col - 1,)), dma((n_col - 1,)),
            dma((n_pan - 1,)), dma((n_pan - 1,)),
        ],
        compiler_params=pltpu.CompilerParams(
            collective_id=1, has_side_effects=True, vmem_limit_bytes=40 * 1024 * 1024
        ),
    )(*parts, rows_t, inv)


def shards(panel_rows, diag_blocks, adjoint, fill):
    n_col = lax.axis_size("col")
    n_pan = lax.axis_size("panel")
    groups = n_pan // n_col
    pairs = []
    for c in range(n_col):
        for k in range(groups):
            for z in range(n_col):
                pairs.append(((groups * c + k) * n_col + z, (k * n_col + z) * n_col + c))
    moved = lax.ppermute(panel_rows, ("panel", "col"), pairs)
    inv = inverse(0.5 * (diag_blocks + diag_blocks.T))
    columns = collect(moved)
    piece = panel_rows.shape[0]
    col = lax.axis_index("col")
    parts = []
    for k in range(n_col - 1, -1, -1):
        start = lax.rem(col + k, n_col) * (piece // B)
        part = multiply(start.astype(jnp.int32)[None], piece, fill, adjoint, columns)
        if k:
            part = lax.ppermute(part, "col", [(c, (c + k) % n_col) for c in range(n_col)])
        parts.append(part)
    return finish(parts, panel_rows.T, inv)


def solution(mesh):
    in_specs = (P(("panel", "col"), None), P(), P("panel", "col"), P("panel", "col"))
    out_specs = (P(("panel", "col"), None), P())
    return jax.shard_map(shards, mesh=mesh, in_specs=in_specs, out_specs=out_specs, check_vma=False)
```
